32 devices in a mesh: fsdp: 16 (over z, y, x), ctx: 2 (over core).
Axes of the slice: x: 2, y: 2, z: 4, core: 2. Of those that a mesh axis runs over, the one named last changes fastest.
Arguments:
- tokens: bfloat16 [15360, 576], P(('fsdp', 'ctx')), may hold values from -6 to 6
- segments: int32 [15360], P('fsdp'), may hold values from 0 to 3, as said below
- gains: bfloat16 [2, 576], P(None, 'ctx'), may hold values from 0.099609375 to 1.8984375
- w_query: bfloat16 [331776], P(('fsdp', 'ctx')), may hold values from -0.25 to 0.25
- w_key: bfloat16 [110592], P(('fsdp', 'ctx')), may hold values from -0.25 to 0.25
- w_value: bfloat16 [110592], P(('fsdp', 'ctx')), may hold values from -0.25 to 0.25
- w_out: bfloat16 [331776], P(('fsdp', 'ctx')), may hold values from -2 to 2
- w_gate: bfloat16 [884736], P(('fsdp', 'ctx')), may hold values from -0.25 to 0.25
- w_up: bfloat16 [884736], P(('fsdp', 'ctx')), may hold values from -0.25 to 0.25
- w_down: bfloat16 [884736], P(('fsdp', 'ctx')), may hold values from -0.3125 to 0.3125
- cotangent: bfloat16 [15360, 576], P(('fsdp', 'ctx')), may hold values from -7.2 to 7.2
Outputs:
- activations: float32 [15360, 576], P(('fsdp', 'ctx'))
- token_grad: float32 [15360, 576], P(('fsdp', 'ctx'))
- gains_grad: float32 [2, 576], P(None, 'ctx')
- query_grad: float32 [331776], P(('fsdp', 'ctx'))
- key_grad: float32 [110592], P(('fsdp', 'ctx'))
- value_grad: float32 [110592], P(('fsdp', 'ctx'))
- out_grad: float32 [331776], P(('fsdp', 'ctx'))
- gate_grad: float32 [884736], P(('fsdp', 'ctx'))
- up_grad: float32 [884736], P(('fsdp', 'ctx'))
- down_grad: float32 [884736], P(('fsdp', 'ctx'))
The draws below stay inside these ranges and needn't reach their ends.
Inputs may be any that keep to these rules, and one draw needn't show every extreme that they name: `segments`: within each sequence of 960 tokens the ids start at 0, never fall and rise by at most one from a token to the next; no document starts at place 960 // 2 of a sequence.
All inputs are finite; a program needn't handle non-finite values.
Results may differ from the reference program's by a relative error of at most 0.015.
Values may be sent and summed in bfloat16 or wider, within the bound.
A program may use at most 128 MiB of HBM per device.

```python
import math
import jax
import jax.numpy as jnp
from jax import lax

D = 576
HEADS = 9
KV_HEADS = 3
HEAD_DIM = 64
FF = 1536
SEQ_LEN = 960
TOKENS = 15360


def draw_segments(key, part):
    key = jax.random.fold_in(key, 11)
    seq_count = TOKENS // SEQ_LEN
    shortest = max(1, SEQ_LEN * 200 // 512)
    longest = max(shortest + 1, SEQ_LEN * 2000 // 512)
    first_key, rest_key, pick_key = jax.random.split(key, 3)
    first_len = jax.random.randint(first_key, (seq_count, 1), 1, longest + 1, dtype=jnp.int32)
    rest_len = jax.random.randint(rest_key, (seq_count, 7), shortest, longest + 1, dtype=jnp.int32)
    lengths = jnp.concatenate([first_len, rest_len], 1)
    chosen = jax.random.randint(pick_key, (), 0, seq_count, dtype=jnp.int32)
    forced = jnp.concatenate([jnp.ones((1,), jnp.int32), jnp.full((7,), shortest, jnp.int32)])
    is_chosen = jnp.arange(seq_count, dtype=jnp.int32)[:, None] == chosen
    lengths = jnp.where(is_chosen, forced[None, :], lengths)
    bounds = jnp.cumsum(lengths, axis=1)
    places = jnp.arange(SEQ_LEN, dtype=jnp.int32)
    counted = (bounds[:, None, :] <= places[None, :, None]) & (bounds[:, None, :] != SEQ_LEN // 2)
    seg_ids = jnp.sum(counted.astype(jnp.int32), 2)
    return seg_ids.reshape(TOKENS).astype(jnp.int32)


def draw_cotangent(key, part):
    key = jax.random.fold_in(key, 7)
    ramp = 3.0 ** (jnp.arange(TOKENS, dtype=jnp.float32) / (TOKENS - 1))
    base = jnp.clip(jax.random.normal(key, (TOKENS, D), jnp.float32), -4.0, 4.0)
    return (base * ramp[:, None] * 0.6).astype(jnp.bfloat16)


def steps_of(own_key, shape, cuts, smallest, high):
    loudness, own = 1.0, jax.random.fold_in(own_key, 6)
    for axis_at, parts in cuts:
        heights = jnp.exp(jax.random.uniform(jax.random.fold_in(own, axis_at), (parts,), jnp.float32, smallest / len(cuts), high / len(cuts)))
        loudness = loudness * jnp.repeat(heights, shape[axis_at] // parts).reshape([-1 if axis == axis_at else 1 for axis in range(len(shape))])
    return loudness


def normal_values(key, extent, spread, limit, cuts=(), held_as=jnp.bfloat16):
    drawn = spread * jax.random.normal(key, extent, jnp.float32)
    if cuts:
        drawn = drawn * steps_of(key, extent, cuts, -0.22, 0.18)
    return jnp.clip(drawn, -limit, limit).astype(held_as)


def setup_inputs(seed: int = 0) -> dict:
    splits = jax.random.split(jax.random.key(seed), 12)
    tokens = normal_values(splits[0], (TOKENS, D), 1.0, 6.0, ((0, 32),))
    segments = draw_segments(jax.random.fold_in(splits[11], 71), 0)
    gains = jnp.clip(1.0 + 0.18 * jax.random.normal(splits[2], (2, D), jnp.float32), 0.099609375, 1.8984375).astype(jnp.bfloat16)
    w_query = normal_values(splits[3], (D * D,), D ** -0.5, 0.25, ((0, 32),))
    w_key = normal_values(splits[4], (D * KV_HEADS * HEAD_DIM,), D ** -0.5, 0.25, ((0, 32),))
    w_value = normal_values(splits[5], (D * KV_HEADS * HEAD_DIM,), D ** -0.5, 0.25, ((0, 32),))
    w_out = normal_values(splits[6], (D * D,), (D // 64) ** -0.5, 2.0, ((0, 32),))
    w_gate = normal_values(splits[7], (D * FF,), D ** -0.5, 0.25, ((0, 32),))
    w_up = normal_values(splits[8], (D * FF,), D ** -0.5, 0.25, ((0, 32),))
    w_down = normal_values(splits[9], (FF * D,), (FF // 4) ** -0.5, 0.3125, ((0, 32),))
    cotangent = draw_cotangent(jax.random.fold_in(splits[11], 71), 0)
    return dict(tokens=tokens, segments=segments, gains=gains, w_query=w_query, w_key=w_key, w_value=w_value, w_out=w_out, w_gate=w_gate, w_up=w_up, w_down=w_down, cotangent=cotangent)


EPS = 1e-05

@jax.custom_vjp
def low(v):
    return lax.optimization_barrier(v.astype(jnp.bfloat16)).astype(jnp.float32)

@jax.custom_vjp
def low_back(v):
    return v

def low_keep(v):
    return (low(v), None)

def low_pass(kept, grad):
    return (grad,)

def back_keep(v):
    return (v, None)

def back_low(kept, grad):
    return (low(grad),)
low.defvjp(low_keep, low_pass)
low_back.defvjp(back_keep, back_low)

def matmul_high(left, right):
    return jnp.dot(left, right, precision=lax.Precision.HIGHEST, preferred_element_type=jnp.float32)

def angle_table(positions):
    inv_freq = 10000.0 ** (-2.0 * jnp.arange(HEAD_DIM // 2, dtype=jnp.float32) / HEAD_DIM)
    angles = positions.astype(jnp.float32)[:, None] * inv_freq[None, :]
    angles = jnp.concatenate([angles, angles], -1)
    return (jnp.cos(angles), jnp.sin(angles))

def rotate(values, cosine, sine_part):
    row_count = values.shape[0]
    heads_view = values.reshape(row_count, -1, HEAD_DIM)
    half_dim = HEAD_DIM // 2
    turned = jnp.concatenate([-heads_view[..., half_dim:], heads_view[..., :half_dim]], -1)
    return (heads_view * cosine[:, None, :] + turned * sine_part[:, None, :]).reshape(row_count, -1)

def one_sequence(tokens_f, seg_ids, gains_f, weights):
    w_query, w_key, w_value, w_out, w_gate, w_up, w_down = weights
    seq_len = tokens_f.shape[0]
    groups = HEADS // KV_HEADS
    norm_one = lax.rsqrt(lax.optimization_barrier(jnp.mean(tokens_f * tokens_f, -1, keepdims=True)) + EPS)
    normed = low(tokens_f * norm_one * gains_f[0])
    queries = low_back(matmul_high(normed, w_query))
    keys = low_back(matmul_high(normed, w_key))
    values = low(low_back(matmul_high(normed, w_value)))
    places = jnp.arange(seq_len, dtype=jnp.int32)
    positions = places - lax.optimization_barrier(jnp.sum((seg_ids[None, :] < seg_ids[:, None]).astype(jnp.int32), 1))
    cosine, sine_part = angle_table(positions)
    q_turned = low(rotate(queries, cosine, sine_part)).reshape(seq_len, KV_HEADS, groups, HEAD_DIM)
    k_turned = low(rotate(keys, cosine, sine_part)).reshape(seq_len, KV_HEADS, HEAD_DIM)
    scores = jnp.einsum('qkgd,skd->kgqs', q_turned, k_turned, precision=lax.Precision.HIGHEST)
    scores = low_back(HEAD_DIM ** (-0.5) * scores)
    allowed = (places[None, :] <= places[:, None]) & (seg_ids[None, :] == seg_ids[:, None])
    scores = jnp.where(allowed[None, None], scores, -1e+30)
    probs = low(jax.nn.softmax(scores, -1))
    mixed = jnp.einsum('kgqs,skd->qkgd', probs, values.reshape(seq_len, KV_HEADS, HEAD_DIM), precision=lax.Precision.HIGHEST).reshape(seq_len, -1)
    mixed = low(low_back(mixed))
    middle = tokens_f + low_back(matmul_high(mixed, w_out))
    norm_two = lax.rsqrt(lax.optimization_barrier(jnp.mean(middle * middle, -1, keepdims=True)) + EPS)
    normed_two = low(middle * norm_two * gains_f[1])
    gate = low_back(matmul_high(normed_two, w_gate))
    upward = low_back(matmul_high(normed_two, w_up))
    hidden = low(jax.nn.silu(gate) * upward)
    return middle + low_back(matmul_high(hidden, w_down))

def reference(tokens, segments, gains, w_query, w_key, w_value, w_out, w_gate, w_up, w_down, cotangent):
    seq_count = TOKENS // SEQ_LEN
    group_size = math.gcd(seq_count, max(1, 4096 // SEQ_LEN))
    seg_blocks = segments.reshape(seq_count // group_size, group_size, SEQ_LEN)

    def forward(tokens_f, gains_f, *flats):
        weights = (flats[0].reshape(D, D), flats[1].reshape(D, -1), flats[2].reshape(D, -1), flats[3].reshape(D, D), flats[4].reshape(D, FF), flats[5].reshape(D, FF), flats[6].reshape(FF, D))
        blocks = tokens_f.reshape(seq_count // group_size, group_size, SEQ_LEN, D)

        def block_step(block_pair):
            return jax.vmap(lambda one_tokens, one_segs: one_sequence(one_tokens, one_segs, gains_f, weights))(block_pair[0], block_pair[1])
        outputs = lax.map(jax.checkpoint(block_step), (blocks, seg_blocks))
        return outputs.reshape(TOKENS, D)
    floats = [matrix.astype(jnp.float32) for matrix in (w_query, w_key, w_value, w_out, w_gate, w_up, w_down)]
    activations, pullback = jax.vjp(forward, tokens.astype(jnp.float32), gains.astype(jnp.float32), *floats)
    grads = pullback(cotangent.astype(jnp.float32))
    return (activations, grads[0], grads[1], grads[2], grads[3], grads[4], grads[5], grads[6], grads[7], grads[8])
```

```python
import jax
import jax.numpy as jnp
import numpy as np
from jax import lax
from jax.sharding import PartitionSpec as P

HEADS = 9
KV_HEADS = 3
HEAD_DIM = 64


EPS = 1e-05


def from_behind(x, axis, by):
    peers = lax.axis_size(axis)
    pairs = [(i, i + by) for i in range(peers) if 0 <= i + by < peers]
    return lax.ppermute(x, axis, pairs)


def angle_table(positions):
    inv_freq = 10000.0 ** (-2.0 * jnp.arange(HEAD_DIM // 2, dtype=jnp.float32) / HEAD_DIM)
    angles = positions.astype(jnp.float32)[:, None] * inv_freq[None, :]
    angles = jnp.concatenate([angles, angles], -1)
    return (jnp.cos(angles), jnp.sin(angles))


def rotate(values, cosine, sine_part):
    row_count = values.shape[0]
    heads_view = values.reshape(row_count, -1, HEAD_DIM)
    half_dim = HEAD_DIM // 2
    turned = jnp.concatenate([-heads_view[..., half_dim:], heads_view[..., :half_dim]], -1)
    return (heads_view * cosine[:, None, :] + turned * sine_part[:, None, :]).reshape(row_count, -1)


def shape_weights(flats, width):
    w_query, w_key, w_value, w_out, w_gate, w_up, w_down = flats
    return (
        w_query.reshape(width, width),
        w_key.reshape(width, -1),
        w_value.reshape(width, -1),
        w_out.reshape(width, width),
        w_gate.reshape(width, -1),
        w_up.reshape(width, -1),
        w_down.reshape(-1, width),
    )


def norm_back(grad_normed, inputs, factor, gain_row):
    scaled = grad_normed * gain_row
    return factor * scaled - inputs * factor**3 * jnp.mean(scaled * inputs, -1, keepdims=True)


def is_power_of_two(n):
    return n & (n - 1) == 0


def swap(x, axis, bit):
    peers = lax.axis_size(axis)
    return lax.ppermute(x, axis, [(i, i ^ (1 << bit)) for i in range(peers)])


def my_bit(axis, bit):
    return (lax.axis_index(axis) >> bit) & 1


def gather_rows(x, order):
    depth = len(order)
    held = x
    for axis, bit in order:
        other = swap(held, axis, bit)
        mine_second = my_bit(axis, bit) == 1
        held = jnp.where(mine_second, jnp.stack([other, held]), jnp.stack([held, other]))
    names = list(reversed(order))
    wanted = sorted(order, key=lambda step: (0 if step[0] == "fsdp" else 1, -step[1]))
    held = held.transpose([names.index(step) for step in wanted] + [depth, depth + 1])
    return held.reshape(-1, x.shape[1])


def scatter_step(held, axis, bit, low):
    half = held.shape[0] // 2
    second = my_bit(axis, bit) == 1
    keep = jnp.where(second, held[half:], held[:half])
    give = jnp.where(second, held[:half], held[half:])
    total = keep.astype(jnp.float32) + swap(give, axis, bit).astype(jnp.float32)
    return total.astype(jnp.bfloat16) if low else total


def scatter_rows(held, order):
    for at, (axis, bit) in enumerate(order):
        held = scatter_step(held, axis, bit, at + 1 < len(order))
    return held


def row_order(order, rows_each, devices):
    places = np.arange(devices * rows_each)
    slot, within = places // rows_each, places % rows_each
    owner = np.zeros_like(slot)
    for at, (axis, bit) in enumerate(order):
        on = (slot >> (len(order) - 1 - at)) & 1
        owner |= on << (bit + 1 if axis == "fsdp" else bit)
    return owner * rows_each + within


def reorder_columns(x, natural):
    picks = (lax.broadcasted_iota(jnp.int32, (x.shape[1], natural.size), 0) == jnp.asarray(natural, jnp.int32)[None, :])
    return jnp.dot(x, picks.astype(jnp.bfloat16), preferred_element_type=jnp.float32).astype(jnp.bfloat16)


def body(tokens, segments, gains, w_query, w_key, w_value, w_out, w_gate, w_up, w_down, cotangent):
    row_count, width = tokens.shape
    groups = HEADS // KV_HEADS
    scale = HEAD_DIM ** (-0.5)
    place = lax.axis_index("ctx")
    first_row = place * row_count
    local_rows = first_row + jnp.arange(row_count, dtype=jnp.int32)
    own_segs = lax.dynamic_slice_in_dim(segments, first_row, row_count)
    positions = local_rows - jnp.sum((segments[None, :] < own_segs[:, None]).astype(jnp.int32), 1)
    padded_segs = jnp.concatenate([jnp.full((row_count,), -1, jnp.int32), segments])
    key_segs = lax.dynamic_slice_in_dim(padded_segs, first_row, 2 * row_count)
    key_rows = first_row - row_count + jnp.arange(2 * row_count, dtype=jnp.int32)
    cosine, sine_part = angle_table(positions)
    block_rows = min(row_count, 512)
    block_count = row_count // block_rows
    gain_full = lax.all_gather(gains, "ctx", axis=1, tiled=True).astype(jnp.float32)
    fsdp_size, ctx_size = lax.axis_size("fsdp"), lax.axis_size("ctx")
    devices = fsdp_size * ctx_size
    kv_width = KV_HEADS * HEAD_DIM
    ff = w_gate.size * devices // width
    row_sizes = ((w_query, width), (w_key, kv_width), (w_out, width), (w_gate, ff), (w_down, width))
    whole_rows = ctx_size == 2 and is_power_of_two(fsdp_size) and all(w.size % columns == 0 for w, columns in row_sizes)
    bits = fsdp_size.bit_length() - 1
    if whole_rows:
        down_bits = [("fsdp", bit) for bit in range(bits - 1, -1, -1)]
        swapped = down_bits[:-2] + down_bits[-2:][::-1]
        order_a, order_b = down_bits + [("ctx", 0)], swapped + [("ctx", 0)]
        first = gather_rows(
            jnp.concatenate([w_query.reshape(-1, width), w_key.reshape(-1, kv_width), w_value.reshape(-1, kv_width), w_out.reshape(-1, width)], 1),
            order_a,
        )
        m_qkv, m_out = first[:, : width + 2 * kv_width], first[:, width + 2 * kv_width :]
        m_gate_up = gather_rows(jnp.concatenate([w_gate.reshape(-1, ff), w_up.reshape(-1, ff)], 1), order_b)
        m_down = gather_rows(w_down.reshape(-1, width), order_a)
    else:
        flats = [lax.all_gather(w, ("fsdp", "ctx"), axis=0, tiled=True) for w in (w_query, w_key, w_value, w_out, w_gate, w_up, w_down)]
        m_query, m_key, m_value, m_out, m_gate, m_up, m_down = shape_weights(flats, width)
        m_qkv = jnp.concatenate([m_query, m_key, m_value], 1)
        m_gate_up = jnp.concatenate([m_gate, m_up], 1)
    tokens_f = tokens.astype(jnp.float32)
    norm_one = lax.rsqrt(jnp.mean(tokens_f * tokens_f, -1, keepdims=True) + EPS)
    normed = (tokens_f * norm_one * gain_full[0]).astype(jnp.bfloat16)
    qkv = jnp.dot(normed, m_qkv, preferred_element_type=jnp.float32)
    queries, keys_raw, values_raw = qkv[:, :width], qkv[:, width : width + kv_width], qkv[:, width + kv_width :]
    q_turned = rotate(queries, cosine, sine_part).astype(jnp.bfloat16)
    k_turned = rotate(keys_raw, cosine, sine_part).astype(jnp.bfloat16)
    v_low = values_raw.astype(jnp.bfloat16)
    far_pair = from_behind(jnp.stack([k_turned, v_low]), "ctx", 1)
    keys_all = jnp.concatenate([far_pair[0], k_turned], 0).reshape(
        2 * row_count, KV_HEADS, HEAD_DIM
    )
    values_all = jnp.concatenate([far_pair[1], v_low], 0).reshape(2 * row_count, KV_HEADS, HEAD_DIM)

    def block_scores(q_block, row_block, seg_block):
        q_heads = q_block.reshape(-1, KV_HEADS, groups, HEAD_DIM)
        raw = (
            jnp.einsum("qkgd,skd->kgqs", q_heads, keys_all, preferred_element_type=jnp.float32)
            * scale
        )
        allowed = (key_rows[None, :] <= row_block[:, None]) & (
            key_segs[None, :] == seg_block[:, None]
        )
        return (q_heads, jnp.where(allowed[None, None], raw, -1e30))

    def attend(block):
        q_block, row_block, seg_block = block
        scores = block_scores(q_block, row_block, seg_block)[1]
        row_max = jnp.max(scores, -1, keepdims=True)
        log_total = row_max + jnp.log(jnp.sum(jnp.exp(scores - row_max), -1, keepdims=True))
        probs_low = jnp.exp(scores - log_total).astype(jnp.bfloat16)
        mixed_block = jnp.einsum(
            "kgqs,skd->qkgd", probs_low, values_all, preferred_element_type=jnp.float32
        )
        return (mixed_block.reshape(q_block.shape[0], -1).astype(jnp.bfloat16), log_total)

    q_blocks = q_turned.reshape(block_count, block_rows, -1)
    row_blocks = local_rows.reshape(block_count, block_rows)
    seg_blocks = own_segs.reshape(block_count, block_rows)
    mixed_blocks, log_totals = lax.map(attend, (q_blocks, row_blocks, seg_blocks))
    mixed = mixed_blocks.reshape(row_count, -1)
    middle = tokens_f + jnp.dot(mixed, m_out, preferred_element_type=jnp.float32)
    norm_two = lax.rsqrt(jnp.mean(middle * middle, -1, keepdims=True) + EPS)
    normed_two = (middle * norm_two * gain_full[1]).astype(jnp.bfloat16)
    gate_up = jnp.dot(normed_two, m_gate_up, preferred_element_type=jnp.float32)
    gate, upward = gate_up[:, :ff], gate_up[:, ff:]
    hidden = (jax.nn.silu(gate) * upward).astype(jnp.bfloat16)
    activations = middle + jnp.dot(hidden, m_down, preferred_element_type=jnp.float32)
    if whole_rows:
        scatter_a = [("ctx", 0)] + [("fsdp", bit) for bit in range(bits)]
        scatter_b = [("ctx", 0)] + [("fsdp", bit) for bit in ((1, 0) if bits > 1 else (0,) * bits)] + [("fsdp", bit) for bit in range(2, bits)]
        rows_each = width // devices
        place_a, place_b = (row_order(order, rows_each, devices) for order in (scatter_a, scatter_b))
        down_rows = ff // devices
        hidden_left = reorder_columns(hidden, row_order(scatter_a, down_rows, devices))
    else:
        hidden_left = hidden
    down_full = jnp.einsum("rf,rd->fd", hidden_left, cotangent, preferred_element_type=jnp.float32)
    if whole_rows:
        down_share = scatter_rows(down_full.astype(jnp.bfloat16), scatter_a)
    grad_hidden = jnp.einsum("rd,fd->rf", cotangent, m_down, preferred_element_type=jnp.float32)
    sigma = jax.nn.sigmoid(gate)
    grad_gate = (grad_hidden * upward * sigma * (1.0 + gate * (1.0 - sigma))).astype(jnp.bfloat16)
    grad_upward = (grad_hidden * gate * sigma).astype(jnp.bfloat16)
    grad_gate_up = jnp.concatenate([grad_gate, grad_upward], 1)
    two_left = reorder_columns(normed_two, place_b) if whole_rows else normed_two
    gate_up_full = jnp.einsum("rd,rf->df", two_left, grad_gate_up, preferred_element_type=jnp.float32)
    grad_normed_two = jnp.einsum("rf,df->rd", grad_gate_up, m_gate_up, preferred_element_type=jnp.float32)
    gain_two_part = jnp.sum(grad_normed_two * middle * norm_two, 0)
    grad_middle = cotangent.astype(jnp.float32) + norm_back(
        grad_normed_two, middle, norm_two, gain_full[1]
    )
    grad_branch = grad_middle.astype(jnp.bfloat16)
    mixed_left = reorder_columns(mixed, place_b) if whole_rows else mixed
    out_full = jnp.einsum("rh,rd->hd", mixed_left, grad_branch, preferred_element_type=jnp.float32)
    grad_mixed = jnp.einsum(
        "rd,hd->rh", grad_branch, m_out, preferred_element_type=jnp.float32
    ).astype(jnp.bfloat16)

    if whole_rows:
        middle_share = scatter_rows(jnp.concatenate([gate_up_full.astype(jnp.bfloat16), out_full.astype(jnp.bfloat16)], 1), scatter_b)

    def back_step(carry, block):
        key_acc, value_acc = carry
        q_block, d_block, lse_block, row_block, seg_block = block
        q_heads, scores = block_scores(q_block, row_block, seg_block)
        probs = jnp.exp(scores - lse_block)
        probs_low = probs.astype(jnp.bfloat16)
        d_heads = d_block.reshape(-1, KV_HEADS, groups, HEAD_DIM)
        grad_probs = jnp.einsum(
            "qkgd,skd->kgqs", d_heads, values_all, preferred_element_type=jnp.float32
        )
        grad_scores = (
            probs * (grad_probs - jnp.sum(probs * grad_probs, -1, keepdims=True))
        ).astype(jnp.bfloat16)
        grad_query = jnp.einsum(
            "kgqs,skd->qkgd", grad_scores, keys_all, preferred_element_type=jnp.float32
        )
        key_acc = (
            key_acc
            + jnp.einsum("kgqs,qkgd->skd", grad_scores, q_heads, preferred_element_type=jnp.float32)
            * scale
        )
        value_acc = value_acc + jnp.einsum(
            "kgqs,qkgd->skd", probs_low, d_heads, preferred_element_type=jnp.float32
        )
        return ((key_acc, value_acc), grad_query.reshape(q_block.shape[0], -1) * scale)

    empty = jnp.zeros((2 * row_count, KV_HEADS, HEAD_DIM), jnp.float32)
    (key_acc, value_acc), grad_q_blocks = lax.scan(
        back_step,
        (empty, empty),
        (
            q_blocks,
            grad_mixed.reshape(block_count, block_rows, -1),
            log_totals,
            row_blocks,
            seg_blocks,
        ),
    )
    far_grads = from_behind(
        jnp.stack([key_acc[:row_count], value_acc[:row_count]]).astype(jnp.bfloat16), "ctx", -1
    ).astype(jnp.float32)
    key_rot_grad = (key_acc[row_count:] + far_grads[0]).reshape(row_count, -1)
    grad_values = (value_acc[row_count:] + far_grads[1]).reshape(row_count, -1).astype(jnp.bfloat16)
    grad_keys = rotate(key_rot_grad, cosine, -sine_part).astype(jnp.bfloat16)
    grad_queries = rotate(grad_q_blocks.reshape(row_count, -1), cosine, -sine_part).astype(
        jnp.bfloat16
    )
    grad_qkv = jnp.concatenate([grad_queries, grad_keys, grad_values], 1)
    one_left = reorder_columns(normed, place_a) if whole_rows else normed
    qkv_full = jnp.einsum("rd,rh->dh", one_left, grad_qkv, preferred_element_type=jnp.float32)
    grad_normed = jnp.einsum("rh,dh->rd", grad_qkv, m_qkv, preferred_element_type=jnp.float32)
    gain_one_part = jnp.sum(grad_normed * tokens_f * norm_one, 0)
    token_grad = grad_middle + norm_back(grad_normed, tokens_f, norm_one, gain_full[0])
    gain_parts = jnp.stack([gain_one_part, gain_two_part])
    splits = (width, width + kv_width)
    if whole_rows:
        qkv_share = scatter_rows(qkv_full.astype(jnp.bfloat16), scatter_a)
        pieces = (*jnp.split(qkv_share, splits, 1), middle_share[:, 2 * ff :], middle_share[:, :ff], middle_share[:, ff : 2 * ff], down_share)
        shares = tuple(piece.reshape(-1) for piece in pieces)
        gains_grad = scatter_step(gain_parts.reshape(2, 2, width // 2).transpose(1, 0, 2), "ctx", 0, False)[0]
        for bit in range(bits):
            gains_grad = gains_grad + swap(gains_grad, "fsdp", bit)
    else:
        fulls = (*jnp.split(qkv_full, splits, 1), out_full, gate_up_full[:, :ff], gate_up_full[:, ff:], down_full)
        shares = tuple(lax.psum_scatter(full.reshape(-1), ("fsdp", "ctx"), scatter_dimension=0, tiled=True) for full in fulls)
        gain_total = lax.psum(gain_parts, ("fsdp", "ctx"))
        gains_grad = lax.dynamic_slice_in_dim(gain_total, place * (width // 2), width // 2, 1)
    return (
        activations,
        token_grad,
        gains_grad,
        shares[0],
        shares[1],
        shares[2],
        shares[3],
        shares[4],
        shares[5],
        shares[6],
    )


def solution(mesh):
    in_specs = (
        P(("fsdp", "ctx"), None),
        P("fsdp"),
        P(None, "ctx"),
        P(("fsdp", "ctx")),
        P(("fsdp", "ctx")),
        P(("fsdp", "ctx")),
        P(("fsdp", "ctx")),
        P(("fsdp", "ctx")),
        P(("fsdp", "ctx")),
        P(("fsdp", "ctx")),
        P(("fsdp", "ctx"), None),
    )
    out_specs = (
        P(("fsdp", "ctx"), None),
        P(("fsdp", "ctx"), None),
        P(None, "ctx"),
        P(("fsdp", "ctx")),
        P(("fsdp", "ctx")),
        P(("fsdp", "ctx")),
        P(("fsdp", "ctx")),
        P(("fsdp", "ctx")),
        P(("fsdp", "ctx")),
        P(("fsdp", "ctx")),
    )
    return jax.shard_map(body, mesh=mesh, in_specs=in_specs, out_specs=out_specs, check_vma=False)
```

```python
import jax
import jax.numpy as jnp
import numpy as np
from jax import lax
from jax.experimental import pallas as pl
from jax.experimental.pallas import tpu as pltpu
from jax.sharding import PartitionSpec as P

HEADS = 9
KV_HEADS = 3
HEAD_DIM = 64


EPS = 1e-05


def from_behind(x, axis, by):
    peers = lax.axis_size(axis)
    pairs = [(i, i + by) for i in range(peers) if 0 <= i + by < peers]
    return lax.ppermute(x, axis, pairs)


def angle_table(positions):
    inv_freq = 10000.0 ** (-2.0 * jnp.arange(HEAD_DIM // 2, dtype=jnp.float32) / HEAD_DIM)
    angles = positions.astype(jnp.float32)[:, None] * inv_freq[None, :]
    angles = jnp.concatenate([angles, angles], -1)
    return (jnp.cos(angles), jnp.sin(angles))


def rotate(values, cosine, sine_part):
    row_count = values.shape[0]
    heads_view = values.reshape(row_count, -1, HEAD_DIM)
    half_dim = HEAD_DIM // 2
    turned = jnp.concatenate([-heads_view[..., half_dim:], heads_view[..., :half_dim]], -1)
    return (heads_view * cosine[:, None, :] + turned * sine_part[:, None, :]).reshape(row_count, -1)


def shape_weights(flats, width):
    w_query, w_key, w_value, w_out, w_gate, w_up, w_down = flats
    return (
        w_query.reshape(width, width),
        w_key.reshape(width, -1),
        w_value.reshape(width, -1),
        w_out.reshape(width, width),
        w_gate.reshape(width, -1),
        w_up.reshape(width, -1),
        w_down.reshape(-1, width),
    )


def norm_back(grad_normed, inputs, factor, gain_row):
    scaled = grad_normed * gain_row
    return factor * scaled - inputs * factor**3 * jnp.mean(scaled * inputs, -1, keepdims=True)


def is_power_of_two(n):
    return n & (n - 1) == 0


def swap(x, axis, bit):
    peers = lax.axis_size(axis)
    return lax.ppermute(x, axis, [(i, i ^ (1 << bit)) for i in range(peers)])


def my_bit(axis, bit):
    return (lax.axis_index(axis) >> bit) & 1


def gather_rows(x, order):
    depth = len(order)
    held = x
    for axis, bit in order:
        other = swap(held, axis, bit)
        mine_second = my_bit(axis, bit) == 1
        held = jnp.where(mine_second, jnp.stack([other, held]), jnp.stack([held, other]))
    names = list(reversed(order))
    wanted = sorted(order, key=lambda step: (0 if step[0] == "fsdp" else 1, -step[1]))
    held = held.transpose([names.index(step) for step in wanted] + [depth, depth + 1])
    return held.reshape(-1, x.shape[1])


def scatter_step(held, axis, bit, low):
    half = held.shape[0] // 2
    second = my_bit(axis, bit) == 1
    keep = jnp.where(second, held[half:], held[:half])
    give = jnp.where(second, held[:half], held[half:])
    total = keep.astype(jnp.float32) + swap(give, axis, bit).astype(jnp.float32)
    return total.astype(jnp.bfloat16) if low else total


def scatter_rows(held, order):
    for at, (axis, bit) in enumerate(order):
        held = scatter_step(held, axis, bit, at + 1 < len(order))
    return held


def row_order(order, rows_each, devices):
    places = np.arange(devices * rows_each)
    slot, within = places // rows_each, places % rows_each
    owner = np.zeros_like(slot)
    for at, (axis, bit) in enumerate(order):
        on = (slot >> (len(order) - 1 - at)) & 1
        owner |= on << (bit + 1 if axis == "fsdp" else bit)
    return owner * rows_each + within


def reorder_columns(x, natural):
    picks = (lax.broadcasted_iota(jnp.int32, (x.shape[1], natural.size), 0) == jnp.asarray(natural, jnp.int32)[None, :])
    return jnp.dot(x, picks.astype(jnp.bfloat16), preferred_element_type=jnp.float32).astype(jnp.bfloat16)


def mask_bias(first_row, row_segs, key_segs, rows):
    key_at = lax.broadcasted_iota(jnp.int32, (2 * rows, rows), 0) - rows
    query_at = lax.broadcasted_iota(jnp.int32, (2 * rows, rows), 1)
    return jnp.where((key_at <= query_at) & (key_segs == row_segs), 0.0, -1e30)


def turn(x):
    return x.astype(jnp.float32).T


def attend_kernel(q_ref, k_ref, v_ref, row_segs_ref, key_segs_ref, mixed_ref, lse_ref, bias_ref):
    rows = q_ref.shape[1]
    groups = HEADS // KV_HEADS
    bias_ref[...] = mask_bias(0, row_segs_ref[...], key_segs_ref[...], rows)
    for kv in range(KV_HEADS):
        keys = k_ref[kv]
        values_t = turn(v_ref[kv]).astype(jnp.bfloat16)
        for head in range(kv * groups, (kv + 1) * groups):
            q_t = q_ref[head * HEAD_DIM : (head + 1) * HEAD_DIM, :]
            scores = jnp.dot(keys, q_t, preferred_element_type=jnp.float32) + bias_ref[...]
            top = jnp.max(scores, 0, keepdims=True)
            raised = jnp.exp(scores - top)
            total = jnp.sum(raised, 0, keepdims=True)
            probs_low = (raised * (1.0 / total)).astype(jnp.bfloat16)
            mixed_t = jnp.dot(values_t, probs_low, preferred_element_type=jnp.float32)
            mixed_ref[head * HEAD_DIM : (head + 1) * HEAD_DIM, :] = mixed_t.astype(jnp.bfloat16)
            lse_ref[head : head + 1, :] = top + jnp.log(total)


def attend(q_t, keys, values, row_segs, key_segs):
    width, rows = q_t.shape
    area = HEADS * rows * 2 * rows
    return pl.pallas_call(
        attend_kernel,
        out_shape=(jax.ShapeDtypeStruct((width, rows), jnp.bfloat16), jax.ShapeDtypeStruct((HEADS, rows), jnp.float32)),
        scratch_shapes=[pltpu.VMEM((2 * rows, rows), jnp.float32)],
        compiler_params=pltpu.CompilerParams(vmem_limit_bytes=40 * 1024 * 1024),
        cost_estimate=pl.CostEstimate(flops=4 * area * HEAD_DIM, bytes_accessed=8 * width * rows, transcendentals=area),
        name="attend",
    )(q_t, keys, values, row_segs, key_segs)


def attend_back_kernel(q_ref, d_ref, lse_ref, k_ref, v_ref, row_segs_ref, key_segs_ref, dq_ref, dk_ref, dv_ref, bias_ref):
    rows = q_ref.shape[1]
    bias_ref[...] = mask_bias(0, row_segs_ref[...], key_segs_ref[...], rows)
    keys, values = k_ref[...], v_ref[...]
    keys_t = (turn(keys) * HEAD_DIM ** (-0.5)).astype(jnp.bfloat16)
    last = (((1,), (1,)), ((), ()))
    for head in range(HEADS // KV_HEADS):
        q_t = q_ref[head * HEAD_DIM : (head + 1) * HEAD_DIM, :]
        d_t = d_ref[head * HEAD_DIM : (head + 1) * HEAD_DIM, :]
        scores = jnp.dot(keys, q_t, preferred_element_type=jnp.float32) + bias_ref[...]
        probs = jnp.exp(scores - lse_ref[head : head + 1, :])
        grad_probs = jnp.dot(values, d_t, preferred_element_type=jnp.float32)
        weighted = probs * grad_probs
        grad_scores = (weighted - probs * jnp.sum(weighted, 0, keepdims=True)).astype(jnp.bfloat16)
        dq_ref[head * HEAD_DIM : (head + 1) * HEAD_DIM, :] = jnp.dot(keys_t, grad_scores, preferred_element_type=jnp.float32)
        dk = lax.dot_general(grad_scores, q_t, last, preferred_element_type=jnp.float32)
        dv = lax.dot_general(probs.astype(jnp.bfloat16), d_t, last, preferred_element_type=jnp.float32)
        dk_ref[...] = dk if head == 0 else dk_ref[...] + dk
        dv_ref[...] = dv if head == 0 else dv_ref[...] + dv


def attend_back(q_t, d_t, lse, keys, values, row_segs, key_segs):
    width, rows = q_t.shape
    area = HEADS // KV_HEADS * rows * 2 * rows
    return pl.pallas_call(
        attend_back_kernel,
        out_shape=(
            jax.ShapeDtypeStruct((width, rows), jnp.float32),
            jax.ShapeDtypeStruct(keys.shape, jnp.float32),
            jax.ShapeDtypeStruct(keys.shape, jnp.float32),
        ),
        scratch_shapes=[pltpu.VMEM((2 * rows, rows), jnp.float32)],
        compiler_params=pltpu.CompilerParams(vmem_limit_bytes=40 * 1024 * 1024),
        cost_estimate=pl.CostEstimate(flops=10 * area * HEAD_DIM, bytes_accessed=16 * width * rows, transcendentals=area),
        name="attend_back",
    )(q_t, d_t, lse, keys, values, row_segs, key_segs)


def body(tokens, segments, gains, w_query, w_key, w_value, w_out, w_gate, w_up, w_down, cotangent):
    row_count, width = tokens.shape
    groups = HEADS // KV_HEADS
    place = lax.axis_index("ctx")
    first_row = place * row_count
    local_rows = first_row + jnp.arange(row_count, dtype=jnp.int32)
    own_segs = lax.dynamic_slice_in_dim(segments, first_row, row_count)
    positions = local_rows - jnp.sum((segments[None, :] < own_segs[:, None]).astype(jnp.int32), 1)
    padded_segs = jnp.concatenate([jnp.full((row_count,), -1, jnp.int32), segments])
    key_segs = lax.dynamic_slice_in_dim(padded_segs, first_row, 2 * row_count)
    cosine, sine_part = angle_table(positions)
    gain_full = lax.all_gather(gains, "ctx", axis=1, tiled=True).astype(jnp.float32)
    fsdp_size, ctx_size = lax.axis_size("fsdp"), lax.axis_size("ctx")
    devices = fsdp_size * ctx_size
    kv_width = KV_HEADS * HEAD_DIM
    ff = w_gate.size * devices // width
    row_sizes = ((w_query, width), (w_key, kv_width), (w_out, width), (w_gate, ff), (w_down, width))
    whole_rows = ctx_size == 2 and is_power_of_two(fsdp_size) and all(w.size % columns == 0 for w, columns in row_sizes)
    bits = fsdp_size.bit_length() - 1
    if whole_rows:
        down_bits = [("fsdp", bit) for bit in range(bits - 1, -1, -1)]
        swapped = down_bits[:-2] + down_bits[-2:][::-1]
        order_a, order_b = down_bits + [("ctx", 0)], swapped + [("ctx", 0)]
        first = gather_rows(
            jnp.concatenate([w_query.reshape(-1, width), w_key.reshape(-1, kv_width), w_value.reshape(-1, kv_width), w_out.reshape(-1, width)], 1),
            order_a,
        )
        m_qkv, m_out = first[:, : width + 2 * kv_width], first[:, width + 2 * kv_width :]
        m_gate_up = gather_rows(jnp.concatenate([w_gate.reshape(-1, ff), w_up.reshape(-1, ff)], 1), order_b)
        m_down = gather_rows(w_down.reshape(-1, width), order_a)
    else:
        flats = [lax.all_gather(w, ("fsdp", "ctx"), axis=0, tiled=True) for w in (w_query, w_key, w_value, w_out, w_gate, w_up, w_down)]
        m_query, m_key, m_value, m_out, m_gate, m_up, m_down = shape_weights(flats, width)
        m_qkv = jnp.concatenate([m_query, m_key, m_value], 1)
        m_gate_up = jnp.concatenate([m_gate, m_up], 1)
    tokens_f = tokens.astype(jnp.float32)
    norm_one = lax.rsqrt(jnp.mean(tokens_f * tokens_f, -1, keepdims=True) + EPS)
    normed = (tokens_f * norm_one * gain_full[0]).astype(jnp.bfloat16)
    qkv = jnp.dot(normed, m_qkv, preferred_element_type=jnp.float32)
    queries, keys_raw, values_raw = qkv[:, :width], qkv[:, width : width + kv_width], qkv[:, width + kv_width :]
    q_turned = rotate(queries, cosine, sine_part).astype(jnp.bfloat16)
    k_turned = rotate(keys_raw, cosine, sine_part).astype(jnp.bfloat16)
    v_low = values_raw.astype(jnp.bfloat16)
    far_pair = from_behind(jnp.stack([k_turned, v_low]), "ctx", 1)
    own_pair = jnp.stack([k_turned, v_low])
    both = jnp.concatenate([far_pair, own_pair], 1).reshape(2, 2 * row_count, KV_HEADS, HEAD_DIM).transpose(0, 2, 1, 3)
    q_scaled_t = (q_turned * HEAD_DIM ** (-0.5)).T
    row_segs, window_segs = own_segs[None, :], key_segs[:, None]
    mixed_t, lse = attend(q_scaled_t, both[0], both[1], row_segs, window_segs)
    mixed = mixed_t.T
    middle = tokens_f + jnp.dot(mixed, m_out, preferred_element_type=jnp.float32)
    norm_two = lax.rsqrt(jnp.mean(middle * middle, -1, keepdims=True) + EPS)
    normed_two = (middle * norm_two * gain_full[1]).astype(jnp.bfloat16)
    gate_up = jnp.dot(normed_two, m_gate_up, preferred_element_type=jnp.float32)
    gate, upward = gate_up[:, :ff], gate_up[:, ff:]
    hidden = (jax.nn.silu(gate) * upward).astype(jnp.bfloat16)
    activations = middle + jnp.dot(hidden, m_down, preferred_element_type=jnp.float32)
    if whole_rows:
        scatter_a = [("ctx", 0)] + [("fsdp", bit) for bit in range(bits)]
        scatter_b = [("ctx", 0)] + [("fsdp", bit) for bit in ((1, 0) if bits > 1 else (0,) * bits)] + [("fsdp", bit) for bit in range(2, bits)]
        rows_each = width // devices
        place_a, place_b = (row_order(order, rows_each, devices) for order in (scatter_a, scatter_b))
        down_rows = ff // devices
        hidden_left = reorder_columns(hidden, row_order(scatter_a, down_rows, devices))
    else:
        hidden_left = hidden
    down_full = jnp.einsum("rf,rd->fd", hidden_left, cotangent, preferred_element_type=jnp.float32)
    grad_hidden = jnp.einsum("rd,fd->rf", cotangent, m_down, preferred_element_type=jnp.float32)
    sigma = jax.nn.sigmoid(gate)
    grad_gate = (grad_hidden * upward * sigma * (1.0 + gate * (1.0 - sigma))).astype(jnp.bfloat16)
    grad_upward = (grad_hidden * gate * sigma).astype(jnp.bfloat16)
    grad_gate_up = jnp.concatenate([grad_gate, grad_upward], 1)
    two_left = reorder_columns(normed_two, place_b) if whole_rows else normed_two
    gate_up_full = jnp.einsum("rd,rf->df", two_left, grad_gate_up, preferred_element_type=jnp.float32)
    grad_normed_two = jnp.einsum("rf,df->rd", grad_gate_up, m_gate_up, preferred_element_type=jnp.float32)
    gain_two_part = jnp.sum(grad_normed_two * middle * norm_two, 0)
    grad_middle = cotangent.astype(jnp.float32) + norm_back(
        grad_normed_two, middle, norm_two, gain_full[1]
    )
    grad_branch = grad_middle.astype(jnp.bfloat16)
    mixed_left = reorder_columns(mixed, place_b) if whole_rows else mixed
    out_full = jnp.einsum("rh,rd->hd", mixed_left, grad_branch, preferred_element_type=jnp.float32)
    grad_mixed_t = jnp.einsum("rd,hd->hr", grad_branch, m_out, preferred_element_type=jnp.float32).astype(jnp.bfloat16)
    group_rows = groups * HEAD_DIM
    sums = []
    if whole_rows:
        down_held = down_full.astype(jnp.bfloat16)
        middle_held = jnp.concatenate([gate_up_full.astype(jnp.bfloat16), out_full.astype(jnp.bfloat16)], 1)
        steps = len(scatter_a)
        down_held = scatter_step(down_held, *scatter_a[0], steps > 1)
        middle_held = scatter_step(middle_held, *scatter_b[0], steps > 1)
        down_held, middle_held, grad_mixed_t = lax.optimization_barrier((down_held, middle_held, grad_mixed_t))
        done = 1
    for kv in range(KV_HEADS):
        at = slice(kv * group_rows, (kv + 1) * group_rows)
        if whole_rows and kv in (0, 2) and done < steps:
            down_held = scatter_step(down_held, *scatter_a[done], done + 1 < steps)
            middle_held = scatter_step(middle_held, *scatter_b[done], done + 1 < steps)
            done += 1
        sums.append(
            attend_back(
                q_scaled_t[at], grad_mixed_t[at], lse[kv * groups : (kv + 1) * groups], both[0, kv], both[1, kv], row_segs, window_segs
            )
        )
        if whole_rows and kv == 1:
            sums, grad_mixed_t, down_held, middle_held = lax.optimization_barrier((sums, grad_mixed_t, down_held, middle_held))
    if whole_rows:
        for step in range(done, steps):
            down_held = scatter_step(down_held, *scatter_a[step], step + 1 < steps)
            middle_held = scatter_step(middle_held, *scatter_b[step], step + 1 < steps)
        down_share, middle_share = down_held, middle_held
    grad_q_t = jnp.concatenate([part[0] for part in sums], 0)
    key_acc = jnp.stack([part[1] for part in sums], 1)
    value_acc = jnp.stack([part[2] for part in sums], 1)
    far_grads = from_behind(
        jnp.stack([key_acc[:row_count], value_acc[:row_count]]).astype(jnp.bfloat16), "ctx", -1
    ).astype(jnp.float32)
    key_rot_grad = (key_acc[row_count:] + far_grads[0]).reshape(row_count, -1)
    grad_values = (value_acc[row_count:] + far_grads[1]).reshape(row_count, -1).astype(jnp.bfloat16)
    grad_keys = rotate(key_rot_grad, cosine, -sine_part).astype(jnp.bfloat16)
    grad_queries = rotate(grad_q_t.T, cosine, -sine_part).astype(
        jnp.bfloat16
    )
    grad_qkv = jnp.concatenate([grad_queries, grad_keys, grad_values], 1)
    one_left = reorder_columns(normed, place_a) if whole_rows else normed
    qkv_full = jnp.einsum("rd,rh->dh", one_left, grad_qkv, preferred_element_type=jnp.float32)
    grad_normed = jnp.einsum("rh,dh->rd", grad_qkv, m_qkv, preferred_element_type=jnp.float32)
    gain_one_part = jnp.sum(grad_normed * tokens_f * norm_one, 0)
    token_grad = grad_middle + norm_back(grad_normed, tokens_f, norm_one, gain_full[0])
    gain_parts = jnp.stack([gain_one_part, gain_two_part])
    splits = (width, width + kv_width)
    if whole_rows:
        qkv_share = scatter_rows(qkv_full.astype(jnp.bfloat16), scatter_a)
        pieces = (*jnp.split(qkv_share, splits, 1), middle_share[:, 2 * ff :], middle_share[:, :ff], middle_share[:, ff : 2 * ff], down_share)
        shares = tuple(piece.reshape(-1) for piece in pieces)
        gains_grad = scatter_step(gain_parts.reshape(2, 2, width // 2).transpose(1, 0, 2), "ctx", 0, False)[0]
        for bit in range(bits):
            gains_grad = gains_grad + swap(gains_grad, "fsdp", bit)
    else:
        fulls = (*jnp.split(qkv_full, splits, 1), out_full, gate_up_full[:, :ff], gate_up_full[:, ff:], down_full)
        shares = tuple(lax.psum_scatter(full.reshape(-1), ("fsdp", "ctx"), scatter_dimension=0, tiled=True) for full in fulls)
        gain_total = lax.psum(gain_parts, ("fsdp", "ctx"))
        gains_grad = lax.dynamic_slice_in_dim(gain_total, place * (width // 2), width // 2, 1)
    return (
        activations,
        token_grad,
        gains_grad,
        shares[0],
        shares[1],
        shares[2],
        shares[3],
        shares[4],
        shares[5],
        shares[6],
    )


def solution(mesh):
    in_specs = (
        P(("fsdp", "ctx"), None),
        P("fsdp"),
        P(None, "ctx"),
        P(("fsdp", "ctx")),
        P(("fsdp", "ctx")),
        P(("fsdp", "ctx")),
        P(("fsdp", "ctx")),
        P(("fsdp", "ctx")),
        P(("fsdp", "ctx")),
        P(("fsdp", "ctx")),
        P(("fsdp", "ctx"), None),
    )
    out_specs = (
        P(("fsdp", "ctx"), None),
        P(("fsdp", "ctx"), None),
        P(None, "ctx"),
        P(("fsdp", "ctx")),
        P(("fsdp", "ctx")),
        P(("fsdp", "ctx")),
        P(("fsdp", "ctx")),
        P(("fsdp", "ctx")),
        P(("fsdp", "ctx")),
        P(("fsdp", "ctx")),
    )
    return jax.shard_map(body, mesh=mesh, in_specs=in_specs, out_specs=out_specs, check_vma=False)
```

```python
import jax
import jax.numpy as jnp
import numpy as np
from jax import lax
from jax.experimental import pallas as pl
from jax.experimental.pallas import tpu as pltpu
from jax.sharding import PartitionSpec as P

HEADS = 9
KV_HEADS = 3
HEAD_DIM = 64


EPS = 1e-05


def from_behind(x, axis, by):
    peers = lax.axis_size(axis)
    pairs = [(i, i + by) for i in range(peers) if 0 <= i + by < peers]
    return lax.ppermute(x, axis, pairs)


def angle_table(positions):
    inv_freq = 10000.0 ** (-2.0 * jnp.arange(HEAD_DIM // 2, dtype=jnp.float32) / HEAD_DIM)
    angles = positions.astype(jnp.float32)[:, None] * inv_freq[None, :]
    angles = jnp.concatenate([angles, angles], -1)
    return (jnp.cos(angles), jnp.sin(angles))


def rotate(values, cosine, sine_part):
    row_count = values.shape[0]
    heads_view = values.reshape(row_count, -1, HEAD_DIM)
    half_dim = HEAD_DIM // 2
    turned = jnp.concatenate([-heads_view[..., half_dim:], heads_view[..., :half_dim]], -1)
    return (heads_view * cosine[:, None, :] + turned * sine_part[:, None, :]).reshape(row_count, -1)


def shape_weights(flats, width):
    w_query, w_key, w_value, w_out, w_gate, w_up, w_down = flats
    return (
        w_query.reshape(width, width),
        w_key.reshape(width, -1),
        w_value.reshape(width, -1),
        w_out.reshape(width, width),
        w_gate.reshape(width, -1),
        w_up.reshape(width, -1),
        w_down.reshape(-1, width),
    )


def norm_back(grad_normed, inputs, factor, gain_row):
    scaled = grad_normed * gain_row
    return factor * scaled - inputs * factor**3 * jnp.mean(scaled * inputs, -1, keepdims=True)


def is_power_of_two(n):
    return n & (n - 1) == 0


def swap(x, axis, bit):
    peers = lax.axis_size(axis)
    return lax.ppermute(x, axis, [(i, i ^ (1 << bit)) for i in range(peers)])


def my_bit(axis, bit):
    return (lax.axis_index(axis) >> bit) & 1


def gather_rows(x, order):
    depth = len(order)
    held = x
    for axis, bit in order:
        other = swap(held, axis, bit)
        mine_second = my_bit(axis, bit) == 1
        held = jnp.where(mine_second, jnp.stack([other, held]), jnp.stack([held, other]))
    names = list(reversed(order))
    wanted = sorted(order, key=lambda step: (0 if step[0] == "fsdp" else 1, -step[1]))
    held = held.transpose([names.index(step) for step in wanted] + [depth, depth + 1])
    return held.reshape(-1, x.shape[1])


def gather_in_step_order(held, order):
    for axis, bit in order:
        other = swap(held, axis, bit)
        mine_second = my_bit(axis, bit) == 1
        held = jnp.where(mine_second, jnp.concatenate([other, held]), jnp.concatenate([held, other]))
    return held


def scatter_step_at(held, axis, bit, low, at):
    second = my_bit(axis, bit) == 1
    lower, upper = lax.index_in_dim(held, 0, at, False), lax.index_in_dim(held, 1, at, False)
    keep, give = jnp.where(second, upper, lower), jnp.where(second, lower, upper)
    total = keep.astype(jnp.float32) + swap(give, axis, bit).astype(jnp.float32)
    return total.astype(jnp.bfloat16) if low else total


def scatter_step(held, axis, bit, low):
    half = held.shape[0] // 2
    second = my_bit(axis, bit) == 1
    keep = jnp.where(second, held[half:], held[:half])
    give = jnp.where(second, held[:half], held[half:])
    total = keep.astype(jnp.float32) + swap(give, axis, bit).astype(jnp.float32)
    return total.astype(jnp.bfloat16) if low else total


def scatter_rows(held, order):
    for at, (axis, bit) in enumerate(order):
        held = scatter_step(held, axis, bit, at + 1 < len(order))
    return held


def row_order(order, rows_each, devices):
    places = np.arange(devices * rows_each)
    slot, within = places // rows_each, places % rows_each
    owner = np.zeros_like(slot)
    for at, (axis, bit) in enumerate(order):
        on = (slot >> (len(order) - 1 - at)) & 1
        owner |= on << (bit + 1 if axis == "fsdp" else bit)
    return owner * rows_each + within


def reorder_rows(x, natural):
    picks = (lax.broadcasted_iota(jnp.int32, (natural.size, x.shape[0]), 1) == jnp.asarray(natural, jnp.int32)[:, None])
    return jnp.dot(picks.astype(jnp.bfloat16), x, preferred_element_type=jnp.float32).astype(jnp.bfloat16)


def reorder_wide(x, natural):
    high = lax.reduce_precision(x, 8, 7)
    terms = jnp.concatenate([high.astype(jnp.bfloat16), (x - high).astype(jnp.bfloat16)], 1)
    picks = (lax.broadcasted_iota(jnp.int32, (x.shape[1], natural.size), 0) == jnp.asarray(natural, jnp.int32)[None, :]).astype(jnp.bfloat16)
    return jnp.dot(terms, jnp.concatenate([picks, picks], 0), preferred_element_type=jnp.float32)


def reorder_columns(x, natural):
    picks = (lax.broadcasted_iota(jnp.int32, (x.shape[1], natural.size), 0) == jnp.asarray(natural, jnp.int32)[None, :])
    return jnp.dot(x, picks.astype(jnp.bfloat16), preferred_element_type=jnp.float32).astype(jnp.bfloat16)


def mask_bias(first_row, row_segs, key_segs, rows):
    key_at = lax.broadcasted_iota(jnp.int32, (2 * rows, rows), 0) - rows
    query_at = lax.broadcasted_iota(jnp.int32, (2 * rows, rows), 1)
    return jnp.where((key_at <= query_at) & (key_segs == row_segs), 0.0, -1e30)


def turn(x):
    return x.astype(jnp.float32).T


def attend_kernel(q_ref, k_ref, v_ref, row_segs_ref, key_segs_ref, mixed_ref, lse_ref, bias_ref):
    rows = q_ref.shape[1]
    groups = HEADS // KV_HEADS
    bias_ref[...] = mask_bias(0, row_segs_ref[...], key_segs_ref[...], rows)
    for kv in range(KV_HEADS):
        keys = k_ref[kv]
        values_t = turn(v_ref[kv]).astype(jnp.bfloat16)
        for head in range(kv * groups, (kv + 1) * groups):
            q_t = q_ref[head * HEAD_DIM : (head + 1) * HEAD_DIM, :]
            scores = jnp.dot(keys, q_t, preferred_element_type=jnp.float32) + bias_ref[...]
            top = jnp.max(scores, 0, keepdims=True)
            raised = jnp.exp(scores - top)
            total = jnp.sum(raised, 0, keepdims=True)
            probs_low = (raised * (1.0 / total)).astype(jnp.bfloat16)
            mixed_t = jnp.dot(values_t, probs_low, preferred_element_type=jnp.float32)
            mixed_ref[head * HEAD_DIM : (head + 1) * HEAD_DIM, :] = mixed_t.astype(jnp.bfloat16)
            lse_ref[head : head + 1, :] = top + jnp.log(total)


def attend(q_t, keys, values, row_segs, key_segs):
    width, rows = q_t.shape
    area = HEADS * rows * 2 * rows
    return pl.pallas_call(
        attend_kernel,
        out_shape=(jax.ShapeDtypeStruct((width, rows), jnp.bfloat16), jax.ShapeDtypeStruct((HEADS, rows), jnp.float32)),
        scratch_shapes=[pltpu.VMEM((2 * rows, rows), jnp.float32)],
        compiler_params=pltpu.CompilerParams(vmem_limit_bytes=40 * 1024 * 1024),
        cost_estimate=pl.CostEstimate(flops=4 * area * HEAD_DIM, bytes_accessed=8 * width * rows, transcendentals=area),
        name="attend",
    )(q_t, keys, values, row_segs, key_segs)


def attend_back_kernel(q_ref, d_ref, lse_ref, k_ref, v_ref, row_segs_ref, key_segs_ref, dq_ref, dk_ref, dv_ref, bias_ref):
    rows = q_ref.shape[1]
    bias_ref[...] = mask_bias(0, row_segs_ref[...], key_segs_ref[...], rows)
    keys, values = k_ref[...], v_ref[...]
    keys_t = (turn(keys) * HEAD_DIM ** (-0.5)).astype(jnp.bfloat16)
    last = (((1,), (1,)), ((), ()))
    for head in range(HEADS // KV_HEADS):
        q_t = q_ref[head * HEAD_DIM : (head + 1) * HEAD_DIM, :]
        d_t = d_ref[head * HEAD_DIM : (head + 1) * HEAD_DIM, :]
        scores = jnp.dot(keys, q_t, preferred_element_type=jnp.float32) + bias_ref[...]
        probs = jnp.exp(scores - lse_ref[head : head + 1, :])
        grad_probs = jnp.dot(values, d_t, preferred_element_type=jnp.float32)
        weighted = probs * grad_probs
        grad_scores = (weighted - probs * jnp.sum(weighted, 0, keepdims=True)).astype(jnp.bfloat16)
        dq_ref[head * HEAD_DIM : (head + 1) * HEAD_DIM, :] = jnp.dot(keys_t, grad_scores, preferred_element_type=jnp.float32)
        dk = lax.dot_general(grad_scores, q_t, last, preferred_element_type=jnp.float32)
        dv = lax.dot_general(probs.astype(jnp.bfloat16), d_t, last, preferred_element_type=jnp.float32)
        dk_ref[...] = dk if head == 0 else dk_ref[...] + dk
        dv_ref[...] = dv if head == 0 else dv_ref[...] + dv


def attend_back(q_t, d_t, lse, keys, values, row_segs, key_segs):
    width, rows = q_t.shape
    area = HEADS // KV_HEADS * rows * 2 * rows
    return pl.pallas_call(
        attend_back_kernel,
        out_shape=(
            jax.ShapeDtypeStruct((width, rows), jnp.float32),
            jax.ShapeDtypeStruct(keys.shape, jnp.float32),
            jax.ShapeDtypeStruct(keys.shape, jnp.float32),
        ),
        scratch_shapes=[pltpu.VMEM((2 * rows, rows), jnp.float32)],
        compiler_params=pltpu.CompilerParams(vmem_limit_bytes=40 * 1024 * 1024),
        cost_estimate=pl.CostEstimate(flops=10 * area * HEAD_DIM, bytes_accessed=16 * width * rows, transcendentals=area),
        name="attend_back",
    )(q_t, d_t, lse, keys, values, row_segs, key_segs)


def body(tokens, segments, gains, w_query, w_key, w_value, w_out, w_gate, w_up, w_down, cotangent):
    row_count, width = tokens.shape
    groups = HEADS // KV_HEADS
    place = lax.axis_index("ctx")
    first_row = place * row_count
    local_rows = first_row + jnp.arange(row_count, dtype=jnp.int32)
    own_segs = lax.dynamic_slice_in_dim(segments, first_row, row_count)
    positions = local_rows - jnp.sum((segments[None, :] < own_segs[:, None]).astype(jnp.int32), 1)
    padded_segs = jnp.concatenate([jnp.full((row_count,), -1, jnp.int32), segments])
    key_segs = lax.dynamic_slice_in_dim(padded_segs, first_row, 2 * row_count)
    cosine, sine_part = angle_table(positions)
    gain_full = lax.all_gather(gains, "ctx", axis=1, tiled=True).astype(jnp.float32)
    fsdp_size, ctx_size = lax.axis_size("fsdp"), lax.axis_size("ctx")
    devices = fsdp_size * ctx_size
    kv_width = KV_HEADS * HEAD_DIM
    ff = w_gate.size * devices // width
    row_sizes = ((w_query, width), (w_key, kv_width), (w_out, width), (w_gate, ff), (w_down, width))
    whole_rows = ctx_size == 2 and is_power_of_two(fsdp_size) and all(w.size % columns == 0 for w, columns in row_sizes)
    bits = fsdp_size.bit_length() - 1
    if whole_rows:
        down_bits = [("fsdp", bit) for bit in range(bits - 1, -1, -1)]
        swapped = down_bits[:-2] + down_bits[-2:][::-1]
        order_a, order_b = down_bits + [("ctx", 0)], swapped + [("ctx", 0)]
        scatter_a, scatter_b = order_a[::-1], order_b[::-1]
        place_a, place_b = (row_order(order, width // devices, devices) for order in (scatter_a, scatter_b))
        back_a, back_b = np.argsort(place_a), np.argsort(place_b)
        m_qkv = gather_in_step_order(
            jnp.concatenate([w_query.reshape(-1, width), w_key.reshape(-1, kv_width), w_value.reshape(-1, kv_width)], 1), order_a
        )
        second = gather_in_step_order(jnp.concatenate([w_gate.reshape(-1, ff), w_up.reshape(-1, ff), w_out.reshape(-1, width)], 1), order_b)
        m_gate_up, m_out = second[:, : 2 * ff], second[:, 2 * ff :]
        m_down = gather_rows(w_down.reshape(-1, width), order_a)
    else:
        flats = [lax.all_gather(w, ("fsdp", "ctx"), axis=0, tiled=True) for w in (w_query, w_key, w_value, w_out, w_gate, w_up, w_down)]
        m_query, m_key, m_value, m_out, m_gate, m_up, m_down = shape_weights(flats, width)
        m_qkv = jnp.concatenate([m_query, m_key, m_value], 1)
        m_gate_up = jnp.concatenate([m_gate, m_up], 1)
    tokens_f = tokens.astype(jnp.float32)
    norm_one = lax.rsqrt(jnp.mean(tokens_f * tokens_f, -1, keepdims=True) + EPS)
    normed = (tokens_f * norm_one * gain_full[0]).astype(jnp.bfloat16)
    one_left = reorder_columns(normed, place_a) if whole_rows else normed
    qkv = jnp.dot(one_left, m_qkv, preferred_element_type=jnp.float32)
    queries, keys_raw, values_raw = qkv[:, :width], qkv[:, width : width + kv_width], qkv[:, width + kv_width :]
    q_turned = rotate(queries, cosine, sine_part).astype(jnp.bfloat16)
    k_turned = rotate(keys_raw, cosine, sine_part).astype(jnp.bfloat16)
    v_low = values_raw.astype(jnp.bfloat16)
    far_pair = from_behind(jnp.stack([k_turned, v_low]), "ctx", 1)
    own_pair = jnp.stack([k_turned, v_low])
    both = jnp.concatenate([far_pair, own_pair], 1).reshape(2, 2 * row_count, KV_HEADS, HEAD_DIM).transpose(0, 2, 1, 3)
    q_scaled_t = (q_turned * HEAD_DIM ** (-0.5)).T
    row_segs, window_segs = own_segs[None, :], key_segs[:, None]
    mixed_t, lse = attend(q_scaled_t, both[0], both[1], row_segs, window_segs)
    mixed_left_t = reorder_rows(mixed_t, place_b) if whole_rows else mixed_t
    middle = tokens_f + jnp.einsum("hr,hd->rd", mixed_left_t, m_out, preferred_element_type=jnp.float32)
    norm_two = lax.rsqrt(jnp.mean(middle * middle, -1, keepdims=True) + EPS)
    normed_two = (middle * norm_two * gain_full[1]).astype(jnp.bfloat16)
    two_left = reorder_columns(normed_two, place_b) if whole_rows else normed_two
    gate_up = jnp.dot(two_left, m_gate_up, preferred_element_type=jnp.float32)
    gate, upward = gate_up[:, :ff], gate_up[:, ff:]
    hidden = (jax.nn.silu(gate) * upward).astype(jnp.bfloat16)
    activations = middle + jnp.dot(hidden, m_down, preferred_element_type=jnp.float32)
    down_full = jnp.einsum("rf,rd->fd", hidden, cotangent, preferred_element_type=jnp.float32)
    grad_hidden = jnp.einsum("rd,fd->rf", cotangent, m_down, preferred_element_type=jnp.float32)
    sigma = jax.nn.sigmoid(gate)
    grad_gate = (grad_hidden * upward * sigma * (1.0 + gate * (1.0 - sigma))).astype(jnp.bfloat16)
    grad_upward = (grad_hidden * gate * sigma).astype(jnp.bfloat16)
    grad_gate_up = jnp.concatenate([grad_gate, grad_upward], 1)
    gate_up_full = jnp.einsum("rd,rf->df", two_left, grad_gate_up, preferred_element_type=jnp.float32)
    grad_normed_two = jnp.einsum("rf,df->rd", grad_gate_up, m_gate_up, preferred_element_type=jnp.float32)
    if whole_rows:
        grad_normed_two = reorder_wide(grad_normed_two, back_b)
    gain_two_part = jnp.sum(grad_normed_two * middle * norm_two, 0)
    grad_middle = cotangent.astype(jnp.float32) + norm_back(
        grad_normed_two, middle, norm_two, gain_full[1]
    )
    grad_branch = grad_middle.astype(jnp.bfloat16)
    out_full = jnp.einsum("hr,rd->hd", mixed_left_t, grad_branch, preferred_element_type=jnp.float32)
    grad_mixed_t = jnp.einsum("rd,hd->hr", grad_branch, m_out, preferred_element_type=jnp.float32).astype(jnp.bfloat16)
    if whole_rows:
        grad_mixed_t = reorder_rows(grad_mixed_t, back_b)
    group_rows = groups * HEAD_DIM
    sums = []
    if whole_rows:
        down_held = down_full.astype(jnp.bfloat16).reshape([2] * (bits + 1) + [-1, width])
        down_at = [bits] + list(range(bits - 1, -1, -1))
        middle_held = jnp.concatenate([gate_up_full.astype(jnp.bfloat16), out_full.astype(jnp.bfloat16)], 1)
        steps = len(scatter_a)
        down_held = scatter_step_at(down_held, *scatter_a[0], steps > 1, down_at[0])
        middle_held = scatter_step(middle_held, *scatter_b[0], steps > 1)
        down_held, middle_held, grad_mixed_t = lax.optimization_barrier((down_held, middle_held, grad_mixed_t))
        done = 1
    for kv in range(KV_HEADS):
        at = slice(kv * group_rows, (kv + 1) * group_rows)
        if whole_rows and kv in (0, 2) and done < steps:
            down_held = scatter_step_at(down_held, *scatter_a[done], done + 1 < steps, down_at[done])
            middle_held = scatter_step(middle_held, *scatter_b[done], done + 1 < steps)
            done += 1
        sums.append(
            attend_back(
                q_scaled_t[at], grad_mixed_t[at], lse[kv * groups : (kv + 1) * groups], both[0, kv], both[1, kv], row_segs, window_segs
            )
        )
        if whole_rows and kv == 1:
            sums, grad_mixed_t, down_held, middle_held = lax.optimization_barrier((sums, grad_mixed_t, down_held, middle_held))
    if whole_rows:
        for step in range(done, steps):
            down_held = scatter_step_at(down_held, *scatter_a[step], step + 1 < steps, down_at[step])
            middle_held = scatter_step(middle_held, *scatter_b[step], step + 1 < steps)
        down_share, middle_share = down_held, middle_held
    grad_q_t = jnp.concatenate([part[0] for part in sums], 0)
    key_acc = jnp.stack([part[1] for part in sums], 1)
    value_acc = jnp.stack([part[2] for part in sums], 1)
    far_grads = from_behind(
        jnp.stack([key_acc[:row_count], value_acc[:row_count]]).astype(jnp.bfloat16), "ctx", -1
    ).astype(jnp.float32)
    key_rot_grad = (key_acc[row_count:] + far_grads[0]).reshape(row_count, -1)
    grad_values = (value_acc[row_count:] + far_grads[1]).reshape(row_count, -1).astype(jnp.bfloat16)
    grad_keys = rotate(key_rot_grad, cosine, -sine_part).astype(jnp.bfloat16)
    grad_queries = rotate(grad_q_t.T, cosine, -sine_part).astype(
        jnp.bfloat16
    )
    grad_qkv = jnp.concatenate([grad_queries, grad_keys, grad_values], 1)
    qkv_full = jnp.einsum("rd,rh->dh", one_left, grad_qkv, preferred_element_type=jnp.float32)
    grad_normed = jnp.einsum("rh,dh->rd", grad_qkv, m_qkv, preferred_element_type=jnp.float32)
    if whole_rows:
        grad_normed = reorder_wide(grad_normed, back_a)
    gain_one_part = jnp.sum(grad_normed * tokens_f * norm_one, 0)
    token_grad = grad_middle + norm_back(grad_normed, tokens_f, norm_one, gain_full[0])
    gain_parts = jnp.stack([gain_one_part, gain_two_part])
    splits = (width, width + kv_width)
    if whole_rows:
        qkv_share = scatter_rows(qkv_full.astype(jnp.bfloat16), scatter_a)
        pieces = (*jnp.split(qkv_share, splits, 1), middle_share[:, 2 * ff :], middle_share[:, :ff], middle_share[:, ff : 2 * ff], down_share)
        shares = tuple(piece.reshape(-1) for piece in pieces)
        gains_grad = scatter_step(gain_parts.reshape(2, 2, width // 2).transpose(1, 0, 2), "ctx", 0, False)[0]
        for bit in range(bits):
            gains_grad = gains_grad + swap(gains_grad, "fsdp", bit)
    else:
        fulls = (*jnp.split(qkv_full, splits, 1), out_full, gate_up_full[:, :ff], gate_up_full[:, ff:], down_full)
        shares = tuple(lax.psum_scatter(full.reshape(-1), ("fsdp", "ctx"), scatter_dimension=0, tiled=True) for full in fulls)
        gain_total = lax.psum(gain_parts, ("fsdp", "ctx"))
        gains_grad = lax.dynamic_slice_in_dim(gain_total, place * (width // 2), width // 2, 1)
    return (
        activations,
        token_grad,
        gains_grad,
        shares[0],
        shares[1],
        shares[2],
        shares[3],
        shares[4],
        shares[5],
        shares[6],
    )


def solution(mesh):
    in_specs = (
        P(("fsdp", "ctx"), None),
        P("fsdp"),
        P(None, "ctx"),
        P(("fsdp", "ctx")),
        P(("fsdp", "ctx")),
        P(("fsdp", "ctx")),
        P(("fsdp", "ctx")),
        P(("fsdp", "ctx")),
        P(("fsdp", "ctx")),
        P(("fsdp", "ctx")),
        P(("fsdp", "ctx"), None),
    )
    out_specs = (
        P(("fsdp", "ctx"), None),
        P(("fsdp", "ctx"), None),
        P(None, "ctx"),
        P(("fsdp", "ctx")),
        P(("fsdp", "ctx")),
        P(("fsdp", "ctx")),
        P(("fsdp", "ctx")),
        P(("fsdp", "ctx")),
        P(("fsdp", "ctx")),
        P(("fsdp", "ctx")),
    )
    return jax.shard_map(body, mesh=mesh, in_specs=in_specs, out_specs=out_specs, check_vma=False)
```

```python
import jax
import jax.numpy as jnp
import numpy as np
from jax import lax
from jax.experimental import pallas as pl
from jax.experimental.pallas import tpu as pltpu
from jax.sharding import PartitionSpec as P

HEADS = 9
KV_HEADS = 3
HEAD_DIM = 64


EPS = 1e-05


def from_behind(x, axis, by):
    peers = lax.axis_size(axis)
    pairs = [(i, i + by) for i in range(peers) if 0 <= i + by < peers]
    return lax.ppermute(x, axis, pairs)


def angle_table(positions):
    inv_freq = 10000.0 ** (-2.0 * jnp.arange(HEAD_DIM // 2, dtype=jnp.float32) / HEAD_DIM)
    angles = positions.astype(jnp.float32)[:, None] * inv_freq[None, :]
    angles = jnp.concatenate([angles, angles], -1)
    return (jnp.cos(angles), jnp.sin(angles))


def rotate(values, cosine, sine_part):
    row_count = values.shape[0]
    heads_view = values.reshape(row_count, -1, HEAD_DIM)
    half_dim = HEAD_DIM // 2
    turned = jnp.concatenate([-heads_view[..., half_dim:], heads_view[..., :half_dim]], -1)
    return (heads_view * cosine[:, None, :] + turned * sine_part[:, None, :]).reshape(row_count, -1)


def shape_weights(flats, width):
    w_query, w_key, w_value, w_out, w_gate, w_up, w_down = flats
    return (
        w_query.reshape(width, width),
        w_key.reshape(width, -1),
        w_value.reshape(width, -1),
        w_out.reshape(width, width),
        w_gate.reshape(width, -1),
        w_up.reshape(width, -1),
        w_down.reshape(-1, width),
    )


def norm_back(grad_normed, inputs, factor, gain_row):
    scaled = grad_normed * gain_row
    return factor * scaled - inputs * factor**3 * jnp.mean(scaled * inputs, -1, keepdims=True)


def is_power_of_two(n):
    return n & (n - 1) == 0


def swap(x, axis, bit):
    peers = lax.axis_size(axis)
    return lax.ppermute(x, axis, [(i, i ^ (1 << bit)) for i in range(peers)])


def my_bit(axis, bit):
    return (lax.axis_index(axis) >> bit) & 1


def gather_rows(x, order):
    depth = len(order)
    held = x
    for axis, bit in order:
        other = swap(held, axis, bit)
        mine_second = my_bit(axis, bit) == 1
        held = jnp.where(mine_second, jnp.stack([other, held]), jnp.stack([held, other]))
    names = list(reversed(order))
    wanted = sorted(order, key=lambda step: (0 if step[0] == "fsdp" else 1, -step[1]))
    held = held.transpose([names.index(step) for step in wanted] + [depth, depth + 1])
    return held.reshape(-1, x.shape[1])


def gather_in_step_order(held, order):
    for axis, bit in order:
        other = swap(held, axis, bit)
        mine_second = my_bit(axis, bit) == 1
        held = jnp.where(mine_second, jnp.concatenate([other, held]), jnp.concatenate([held, other]))
    return held


def in_pairs(order):
    groups = []
    for step in order:
        if groups and len(groups[-1]) == 1 and groups[-1][0][0] == step[0]:
            groups[-1].append(step)
        else:
            groups.append([step])
    return groups


def swap_group(x, group, flips):
    axis = group[0][0]
    mask = sum(1 << bit for at, (_, bit) in enumerate(group) if (flips >> (len(group) - 1 - at)) & 1)
    peers = lax.axis_size(axis)
    return lax.ppermute(x, axis, [(i, i ^ mask) for i in range(peers)])


def slot_of(group):
    slot = 0
    for axis, bit in group:
        slot = slot * 2 + my_bit(axis, bit)
    return slot


def gather_by_groups(held, order):
    for steps in in_pairs(order):
        group = steps[::-1]
        parts = [held] + [swap_group(held, group, flips) for flips in range(1, 1 << len(group))]
        slot = slot_of(group)
        blocks = jnp.stack(parts)
        for level in range(len(group)):
            on = ((slot >> level) & 1) == 1
            turned = jnp.stack([blocks[at ^ (1 << level)] for at in range(len(parts))])
            blocks = jnp.where(on, turned, blocks)
        held = blocks.reshape(-1, held.shape[1])
    return held


def scatter_by_groups(held, order):
    groups = in_pairs(order)
    for at, group in enumerate(groups):
        count = 1 << len(group)
        blocks = held.reshape((count, -1) + held.shape[1:])
        slot = slot_of(group)
        total = lax.dynamic_index_in_dim(blocks, slot, 0, False).astype(jnp.float32)
        gives = [lax.dynamic_index_in_dim(blocks, slot ^ flips, 0, False) for flips in range(1, count)]
        for flips, give in enumerate(gives, 1):
            total = total + swap_group(give, group, flips).astype(jnp.float32)
        held = total.astype(jnp.bfloat16) if at + 1 < len(groups) else total
    return held


def sum_by_groups(x, order):
    for group in in_pairs(order):
        parts = [x] + [swap_group(x, group, flips) for flips in range(1, 1 << len(group))]
        while len(parts) > 1:
            parts = [parts[at] + parts[at + 1] for at in range(0, len(parts), 2)]
        x = parts[0]
    return x


def scatter_step_at(held, axis, bit, low, at):
    second = my_bit(axis, bit) == 1
    lower, upper = lax.index_in_dim(held, 0, at, False), lax.index_in_dim(held, 1, at, False)
    keep, give = jnp.where(second, upper, lower), jnp.where(second, lower, upper)
    total = keep.astype(jnp.float32) + swap(give, axis, bit).astype(jnp.float32)
    return total.astype(jnp.bfloat16) if low else total


def scatter_step(held, axis, bit, low):
    half = held.shape[0] // 2
    second = my_bit(axis, bit) == 1
    keep = jnp.where(second, held[half:], held[:half])
    give = jnp.where(second, held[:half], held[half:])
    total = keep.astype(jnp.float32) + swap(give, axis, bit).astype(jnp.float32)
    return total.astype(jnp.bfloat16) if low else total


def scatter_rows(held, order):
    for at, (axis, bit) in enumerate(order):
        held = scatter_step(held, axis, bit, at + 1 < len(order))
    return held


def row_order(order, rows_each, devices):
    places = np.arange(devices * rows_each)
    slot, within = places // rows_each, places % rows_each
    owner = np.zeros_like(slot)
    for at, (axis, bit) in enumerate(order):
        on = (slot >> (len(order) - 1 - at)) & 1
        owner |= on << (bit + 1 if axis == "fsdp" else bit)
    return owner * rows_each + within


def reorder_rows(x, natural):
    picks = (lax.broadcasted_iota(jnp.int32, (natural.size, x.shape[0]), 1) == jnp.asarray(natural, jnp.int32)[:, None])
    return jnp.dot(picks.astype(jnp.bfloat16), x, preferred_element_type=jnp.float32).astype(jnp.bfloat16)


def reorder_wide(x, natural):
    high = lax.reduce_precision(x, 8, 7)
    terms = jnp.concatenate([high.astype(jnp.bfloat16), (x - high).astype(jnp.bfloat16)], 1)
    picks = (lax.broadcasted_iota(jnp.int32, (x.shape[1], natural.size), 0) == jnp.asarray(natural, jnp.int32)[None, :]).astype(jnp.bfloat16)
    return jnp.dot(terms, jnp.concatenate([picks, picks], 0), preferred_element_type=jnp.float32)


def reorder_columns(x, natural):
    picks = (lax.broadcasted_iota(jnp.int32, (x.shape[1], natural.size), 0) == jnp.asarray(natural, jnp.int32)[None, :])
    return jnp.dot(x, picks.astype(jnp.bfloat16), preferred_element_type=jnp.float32).astype(jnp.bfloat16)


def mask_bias(first_row, row_segs, key_segs, rows):
    key_at = lax.broadcasted_iota(jnp.int32, (2 * rows, rows), 0) - rows
    query_at = lax.broadcasted_iota(jnp.int32, (2 * rows, rows), 1)
    return jnp.where((key_at <= query_at) & (key_segs == row_segs), 0.0, -1e30)


def turn(x):
    return x.astype(jnp.float32).T


def attend_kernel(q_ref, k_ref, v_ref, row_segs_ref, key_segs_ref, mixed_ref, lse_ref, bias_ref):
    rows = q_ref.shape[1]
    groups = HEADS // KV_HEADS
    bias_ref[...] = mask_bias(0, row_segs_ref[...], key_segs_ref[...], rows)
    for kv in range(KV_HEADS):
        keys = k_ref[kv]
        values_t = turn(v_ref[kv]).astype(jnp.bfloat16)
        for head in range(kv * groups, (kv + 1) * groups):
            q_t = q_ref[head * HEAD_DIM : (head + 1) * HEAD_DIM, :]
            scores = jnp.dot(keys, q_t, preferred_element_type=jnp.float32) + bias_ref[...]
            top = jnp.max(scores, 0, keepdims=True)
            raised = jnp.exp(scores - top)
            total = jnp.sum(raised, 0, keepdims=True)
            probs_low = (raised * (1.0 / total)).astype(jnp.bfloat16)
            mixed_t = jnp.dot(values_t, probs_low, preferred_element_type=jnp.float32)
            mixed_ref[head * HEAD_DIM : (head + 1) * HEAD_DIM, :] = mixed_t.astype(jnp.bfloat16)
            lse_ref[head : head + 1, :] = top + jnp.log(total)


def attend(q_t, keys, values, row_segs, key_segs):
    width, rows = q_t.shape
    area = HEADS * rows * 2 * rows
    return pl.pallas_call(
        attend_kernel,
        out_shape=(jax.ShapeDtypeStruct((width, rows), jnp.bfloat16), jax.ShapeDtypeStruct((HEADS, rows), jnp.float32)),
        scratch_shapes=[pltpu.VMEM((2 * rows, rows), jnp.float32)],
        compiler_params=pltpu.CompilerParams(vmem_limit_bytes=40 * 1024 * 1024),
        cost_estimate=pl.CostEstimate(flops=4 * area * HEAD_DIM, bytes_accessed=8 * width * rows, transcendentals=area),
        name="attend",
    )(q_t, keys, values, row_segs, key_segs)


def attend_back_kernel(q_ref, d_ref, lse_ref, k_ref, v_ref, row_segs_ref, key_segs_ref, dq_ref, dk_ref, dv_ref, bias_ref):
    rows = q_ref.shape[1]
    bias_ref[...] = mask_bias(0, row_segs_ref[...], key_segs_ref[...], rows)
    keys, values = k_ref[...], v_ref[...]
    keys_t = (turn(keys) * HEAD_DIM ** (-0.5)).astype(jnp.bfloat16)
    last = (((1,), (1,)), ((), ()))
    for head in range(HEADS // KV_HEADS):
        q_t = q_ref[head * HEAD_DIM : (head + 1) * HEAD_DIM, :]
        d_t = d_ref[head * HEAD_DIM : (head + 1) * HEAD_DIM, :]
        scores = jnp.dot(keys, q_t, preferred_element_type=jnp.float32) + bias_ref[...]
        probs = jnp.exp(scores - lse_ref[head : head + 1, :])
        grad_probs = jnp.dot(values, d_t, preferred_element_type=jnp.float32)
        weighted = probs * grad_probs
        grad_scores = (weighted - probs * jnp.sum(weighted, 0, keepdims=True)).astype(jnp.bfloat16)
        dq_ref[head * HEAD_DIM : (head + 1) * HEAD_DIM, :] = jnp.dot(keys_t, grad_scores, preferred_element_type=jnp.float32)
        dk = lax.dot_general(grad_scores, q_t, last, preferred_element_type=jnp.float32)
        dv = lax.dot_general(probs.astype(jnp.bfloat16), d_t, last, preferred_element_type=jnp.float32)
        dk_ref[...] = dk if head == 0 else dk_ref[...] + dk
        dv_ref[...] = dv if head == 0 else dv_ref[...] + dv


def attend_back(q_t, d_t, lse, keys, values, row_segs, key_segs):
    width, rows = q_t.shape
    area = HEADS // KV_HEADS * rows * 2 * rows
    return pl.pallas_call(
        attend_back_kernel,
        out_shape=(
            jax.ShapeDtypeStruct((width, rows), jnp.float32),
            jax.ShapeDtypeStruct(keys.shape, jnp.float32),
            jax.ShapeDtypeStruct(keys.shape, jnp.float32),
        ),
        scratch_shapes=[pltpu.VMEM((2 * rows, rows), jnp.float32)],
        compiler_params=pltpu.CompilerParams(vmem_limit_bytes=40 * 1024 * 1024),
        cost_estimate=pl.CostEstimate(flops=10 * area * HEAD_DIM, bytes_accessed=16 * width * rows, transcendentals=area),
        name="attend_back",
    )(q_t, d_t, lse, keys, values, row_segs, key_segs)


def body(tokens, segments, gains, w_query, w_key, w_value, w_out, w_gate, w_up, w_down, cotangent):
    row_count, width = tokens.shape
    groups = HEADS // KV_HEADS
    place = lax.axis_index("ctx")
    first_row = place * row_count
    local_rows = first_row + jnp.arange(row_count, dtype=jnp.int32)
    own_segs = lax.dynamic_slice_in_dim(segments, first_row, row_count)
    positions = local_rows - jnp.sum((segments[None, :] < own_segs[:, None]).astype(jnp.int32), 1)
    padded_segs = jnp.concatenate([jnp.full((row_count,), -1, jnp.int32), segments])
    key_segs = lax.dynamic_slice_in_dim(padded_segs, first_row, 2 * row_count)
    cosine, sine_part = angle_table(positions)
    gain_full = lax.all_gather(gains, "ctx", axis=1, tiled=True).astype(jnp.float32)
    fsdp_size, ctx_size = lax.axis_size("fsdp"), lax.axis_size("ctx")
    devices = fsdp_size * ctx_size
    kv_width = KV_HEADS * HEAD_DIM
    ff = w_gate.size * devices // width
    row_sizes = ((w_query, width), (w_key, kv_width), (w_out, width), (w_gate, ff), (w_down, width))
    whole_rows = ctx_size == 2 and is_power_of_two(fsdp_size) and all(w.size % columns == 0 for w, columns in row_sizes)
    bits = fsdp_size.bit_length() - 1
    if whole_rows:
        down_bits = [("fsdp", bit) for bit in range(bits - 1, -1, -1)]
        swapped = down_bits[:-2] + down_bits[-2:][::-1]
        order_a, order_b = down_bits + [("ctx", 0)], swapped + [("ctx", 0)]
        scatter_a, scatter_b = order_a[::-1], order_b[::-1]
        place_a, place_b = (row_order(order, width // devices, devices) for order in (scatter_a, scatter_b))
        back_a, back_b = np.argsort(place_a), np.argsort(place_b)
        m_qkv = gather_by_groups(
            jnp.concatenate([w_query.reshape(-1, width), w_key.reshape(-1, kv_width), w_value.reshape(-1, kv_width)], 1), order_a
        )
        second = jnp.concatenate([w_gate.reshape(-1, ff), w_up.reshape(-1, ff), w_out.reshape(-1, width)], 1)
        second = gather_in_step_order(second, order_b[:-2])
        second_other = swap(second, *order_b[-2])
        m_down = gather_rows(w_down.reshape(-1, width), order_a)
    else:
        flats = [lax.all_gather(w, ("fsdp", "ctx"), axis=0, tiled=True) for w in (w_query, w_key, w_value, w_out, w_gate, w_up, w_down)]
        m_query, m_key, m_value, m_out, m_gate, m_up, m_down = shape_weights(flats, width)
        m_qkv = jnp.concatenate([m_query, m_key, m_value], 1)
        m_gate_up = jnp.concatenate([m_gate, m_up], 1)
    tokens_f = tokens.astype(jnp.float32)
    norm_one = lax.rsqrt(jnp.mean(tokens_f * tokens_f, -1, keepdims=True) + EPS)
    normed = (tokens_f * norm_one * gain_full[0]).astype(jnp.bfloat16)
    one_left = reorder_columns(normed, place_a) if whole_rows else normed
    qkv = jnp.dot(one_left, m_qkv, preferred_element_type=jnp.float32)
    queries, keys_raw, values_raw = qkv[:, :width], qkv[:, width : width + kv_width], qkv[:, width + kv_width :]
    q_turned = rotate(queries, cosine, sine_part).astype(jnp.bfloat16)
    k_turned = rotate(keys_raw, cosine, sine_part).astype(jnp.bfloat16)
    v_low = values_raw.astype(jnp.bfloat16)
    far_pair = from_behind(jnp.stack([k_turned, v_low]), "ctx", 1)
    own_pair = jnp.stack([k_turned, v_low])
    both = jnp.concatenate([far_pair, own_pair], 1).reshape(2, 2 * row_count, KV_HEADS, HEAD_DIM).transpose(0, 2, 1, 3)
    q_scaled_t = (q_turned * HEAD_DIM ** (-0.5)).T
    row_segs, window_segs = own_segs[None, :], key_segs[:, None]
    if whole_rows:
        q_scaled_t, both, second, second_other = lax.optimization_barrier((q_scaled_t, both, second, second_other))
        mine_second = my_bit(*order_b[-2]) == 1
        second = jnp.where(mine_second, jnp.concatenate([second_other, second]), jnp.concatenate([second, second_other]))
        second = gather_in_step_order(second, order_b[-1:])
        m_gate_up, m_out = second[:, : 2 * ff], second[:, 2 * ff :]
    mixed_t, lse = attend(q_scaled_t, both[0], both[1], row_segs, window_segs)
    mixed_left_t = reorder_rows(mixed_t, place_b) if whole_rows else mixed_t
    middle = tokens_f + jnp.einsum("hr,hd->rd", mixed_left_t, m_out, preferred_element_type=jnp.float32)
    norm_two = lax.rsqrt(jnp.mean(middle * middle, -1, keepdims=True) + EPS)
    normed_two = (middle * norm_two * gain_full[1]).astype(jnp.bfloat16)
    two_left = reorder_columns(normed_two, place_b) if whole_rows else normed_two
    gate_up = jnp.dot(two_left, m_gate_up, preferred_element_type=jnp.float32)
    gate, upward = gate_up[:, :ff], gate_up[:, ff:]
    hidden = (jax.nn.silu(gate) * upward).astype(jnp.bfloat16)
    activations = middle + jnp.dot(hidden, m_down, preferred_element_type=jnp.float32)
    down_full = jnp.einsum("rf,rd->fd", hidden, cotangent, preferred_element_type=jnp.float32)
    grad_hidden = jnp.einsum("rd,fd->rf", cotangent, m_down, preferred_element_type=jnp.float32)
    sigma = jax.nn.sigmoid(gate)
    grad_gate = (grad_hidden * upward * sigma * (1.0 + gate * (1.0 - sigma))).astype(jnp.bfloat16)
    grad_upward = (grad_hidden * gate * sigma).astype(jnp.bfloat16)
    grad_gate_up = jnp.concatenate([grad_gate, grad_upward], 1)
    gate_up_full = jnp.einsum("rd,rf->df", two_left, grad_gate_up, preferred_element_type=jnp.float32)
    grad_normed_two = jnp.einsum("rf,df->rd", grad_gate_up, m_gate_up, preferred_element_type=jnp.float32)
    if whole_rows:
        grad_normed_two = reorder_wide(grad_normed_two, back_b)
    gain_two_part = jnp.sum(grad_normed_two * middle * norm_two, 0)
    grad_middle = cotangent.astype(jnp.float32) + norm_back(
        grad_normed_two, middle, norm_two, gain_full[1]
    )
    grad_branch = grad_middle.astype(jnp.bfloat16)
    out_full = jnp.einsum("hr,rd->hd", mixed_left_t, grad_branch, preferred_element_type=jnp.float32)
    grad_mixed_t = jnp.einsum("rd,hd->hr", grad_branch, m_out, preferred_element_type=jnp.float32).astype(jnp.bfloat16)
    if whole_rows:
        grad_mixed_t = reorder_rows(grad_mixed_t, back_b)
    group_rows = groups * HEAD_DIM
    sums = []
    if whole_rows:
        down_held = down_full.astype(jnp.bfloat16).reshape([2] * (bits + 1) + [-1, width])
        down_at = [bits] + list(range(bits - 1, -1, -1))
        middle_held = jnp.concatenate([gate_up_full.astype(jnp.bfloat16), out_full.astype(jnp.bfloat16)], 1)
        steps = len(scatter_a)
        down_held = scatter_step_at(down_held, *scatter_a[0], steps > 1, down_at[0])
        middle_held = scatter_step(middle_held, *scatter_b[0], steps > 1)
        down_held, middle_held, grad_mixed_t = lax.optimization_barrier((down_held, middle_held, grad_mixed_t))
        done = 1
    for kv in range(KV_HEADS):
        at = slice(kv * group_rows, (kv + 1) * group_rows)
        if whole_rows and kv in (0, 2) and done < steps:
            down_held = scatter_step_at(down_held, *scatter_a[done], done + 1 < steps, down_at[done])
            middle_held = scatter_step(middle_held, *scatter_b[done], done + 1 < steps)
            done += 1
        sums.append(
            attend_back(
                q_scaled_t[at], grad_mixed_t[at], lse[kv * groups : (kv + 1) * groups], both[0, kv], both[1, kv], row_segs, window_segs
            )
        )
        if whole_rows and kv == 1:
            sums, grad_mixed_t, down_held, middle_held = lax.optimization_barrier((sums, grad_mixed_t, down_held, middle_held))
    if whole_rows:
        for step in range(done, steps):
            down_held = scatter_step_at(down_held, *scatter_a[step], step + 1 < steps, down_at[step])
            middle_held = scatter_step(middle_held, *scatter_b[step], step + 1 < steps)
        down_share, middle_share = down_held, middle_held
    grad_q_t = jnp.concatenate([part[0] for part in sums], 0)
    key_acc = jnp.stack([part[1] for part in sums], 1)
    value_acc = jnp.stack([part[2] for part in sums], 1)
    far_grads = from_behind(
        jnp.stack([key_acc[:row_count], value_acc[:row_count]]).astype(jnp.bfloat16), "ctx", -1
    ).astype(jnp.float32)
    key_rot_grad = (key_acc[row_count:] + far_grads[0]).reshape(row_count, -1)
    grad_values = (value_acc[row_count:] + far_grads[1]).reshape(row_count, -1).astype(jnp.bfloat16)
    grad_keys = rotate(key_rot_grad, cosine, -sine_part).astype(jnp.bfloat16)
    grad_queries = rotate(grad_q_t.T, cosine, -sine_part).astype(
        jnp.bfloat16
    )
    grad_qkv = jnp.concatenate([grad_queries, grad_keys, grad_values], 1)
    qkv_full = jnp.einsum("rd,rh->dh", one_left, grad_qkv, preferred_element_type=jnp.float32)
    grad_normed = jnp.einsum("rh,dh->rd", grad_qkv, m_qkv, preferred_element_type=jnp.float32)
    if whole_rows:
        grad_normed = reorder_wide(grad_normed, back_a)
    gain_one_part = jnp.sum(grad_normed * tokens_f * norm_one, 0)
    token_grad = grad_middle + norm_back(grad_normed, tokens_f, norm_one, gain_full[0])
    gain_parts = jnp.stack([gain_one_part, gain_two_part])
    splits = (width, width + kv_width)
    if whole_rows:
        qkv_share = scatter_by_groups(qkv_full.astype(jnp.bfloat16), scatter_a)
        pieces = (*jnp.split(qkv_share, splits, 1), middle_share[:, 2 * ff :], middle_share[:, :ff], middle_share[:, ff : 2 * ff], down_share)
        shares = tuple(piece.reshape(-1) for piece in pieces)
        gains_grad = scatter_step(gain_parts.reshape(2, 2, width // 2).transpose(1, 0, 2), "ctx", 0, False)[0]
        gains_grad = sum_by_groups(gains_grad, scatter_a[1:])
    else:
        fulls = (*jnp.split(qkv_full, splits, 1), out_full, gate_up_full[:, :ff], gate_up_full[:, ff:], down_full)
        shares = tuple(lax.psum_scatter(full.reshape(-1), ("fsdp", "ctx"), scatter_dimension=0, tiled=True) for full in fulls)
        gain_total = lax.psum(gain_parts, ("fsdp", "ctx"))
        gains_grad = lax.dynamic_slice_in_dim(gain_total, place * (width // 2), width // 2, 1)
    return (
        activations,
        token_grad,
        gains_grad,
        shares[0],
        shares[1],
        shares[2],
        shares[3],
        shares[4],
        shares[5],
        shares[6],
    )


def solution(mesh):
    in_specs = (
        P(("fsdp", "ctx"), None),
        P("fsdp"),
        P(None, "ctx"),
        P(("fsdp", "ctx")),
        P(("fsdp", "ctx")),
        P(("fsdp", "ctx")),
        P(("fsdp", "ctx")),
        P(("fsdp", "ctx")),
        P(("fsdp", "ctx")),
        P(("fsdp", "ctx")),
        P(("fsdp", "ctx"), None),
    )
    out_specs = (
        P(("fsdp", "ctx"), None),
        P(("fsdp", "ctx"), None),
        P(None, "ctx"),
        P(("fsdp", "ctx")),
        P(("fsdp", "ctx")),
        P(("fsdp", "ctx")),
        P(("fsdp", "ctx")),
        P(("fsdp", "ctx")),
        P(("fsdp", "ctx")),
        P(("fsdp", "ctx")),
    )
    return jax.shard_map(body, mesh=mesh, in_specs=in_specs, out_specs=out_specs, check_vma=False)
```
